128 devices in a mesh: replica: 8 (over z, core), fsdp: 16 (over y, x).
Axes of the slice: x: 4, y: 4, z: 4, core: 2. Of those that a mesh axis runs over, the one named last changes fastest.
Arguments:
- outer_grad: bfloat16 [8, 4096, 14336], P('replica', 'fsdp'), may hold values from -64 to 64
- error_prev: bfloat16 [8, 4096, 14336], P('replica', 'fsdp'), may hold values from -6 to 6
- q_init: float32 [8, 14336], replicated, may hold values from -6 to 6
Outputs:
- update: bfloat16 [4096, 14336], P('fsdp', 'replica')
- new_error: bfloat16 [8, 4096, 14336], P('replica', 'fsdp')
The draws below stay inside these ranges and needn't reach their ends.
All inputs are finite; a program needn't handle non-finite values.
Results may differ from the reference program's by a relative error of at most 0.0011.
Values sent between devices are 32-bit elements; how exact they have to be, the bound alone decides.
A program may use at most 128 MiB of HBM per device.

```python
import math
import jax
import jax.numpy as jnp
from jax import lax

ROWS = 4096
COLS = 14336
RANK = 8
ITERS = 2
REPLICAS = 8
N_REPLICA = 8


def draw_outer_grad(key, part):
    key = jax.random.fold_in(key, 11)
    key_base, key_rows, key_cols = jax.random.split(key, 3)
    frac = jnp.arange(ROWS, dtype=jnp.float32) / ROWS
    row_scale = jnp.power(3.0, frac) * jnp.exp(jax.random.uniform(key_rows, (ROWS,), jnp.float32, math.log(0.4), math.log(1.3)))
    col_scale = jnp.exp(jax.random.uniform(key_cols, (COLS,), jnp.float32, math.log(0.4), math.log(4.0)))
    base = jnp.clip(jax.random.normal(key_base, (REPLICAS, ROWS, COLS), jnp.float32), -4.0, 4.0)
    return (base * row_scale[None, :, None] * col_scale[None, None, :]).astype(jnp.bfloat16)


def steps_of(stream_key, shape, pieces, smallest, largest):
    def one(dim, shards_of):
        heights = jax.random.uniform(jax.random.fold_in(jax.random.fold_in(stream_key, 6), dim), (shards_of,), jnp.float32, smallest / len(pieces), largest / len(pieces))
        return jnp.repeat(jnp.exp(heights), shape[dim] // shards_of).reshape((-1,) + (1,) * (len(shape) - dim - 1))

    level = one(*pieces[0])
    for cut in pieces[1:]:
        level = level * one(*cut)
    return level


def normal_values(rng, shape, spread, bound, pieces=(), kind=jnp.bfloat16):
    drawn = spread * jax.random.normal(rng, shape, jnp.float32)
    if pieces:
        drawn = drawn * steps_of(rng, shape, pieces, -0.22, 0.18)
    return jnp.clip(drawn, -bound, bound).astype(kind)


def setup_inputs(seed: int = 0) -> dict:
    streams_of = jax.random.split(jax.random.key(seed), 4)
    return {
        "outer_grad": draw_outer_grad(jax.random.fold_in(streams_of[3], 71), 0),
        "error_prev": normal_values(streams_of[1], (REPLICAS, ROWS, COLS), 1.0, 6.0, ((0, 8), (1, 16))),
        "q_init": normal_values(streams_of[2], (RANK, COLS), 1.0, 6.0, (), jnp.float32),
    }


HIGHEST = lax.Precision.HIGHEST

def normalize(image):
    gram = lax.dot_general(image, image, (((0,), (0,)), ((), ())), precision=HIGHEST)
    lower = jnp.linalg.cholesky(gram)
    solved = lax.linalg.triangular_solve(lower, image.T, left_side=True, lower=True)
    return solved.T

def reference(outer_grad, error_prev, q_init):
    errors = []
    total = jnp.zeros((ROWS, COLS), jnp.float32)
    for replica_index in range(N_REPLICA):
        merged = outer_grad[replica_index].astype(jnp.float32) + error_prev[replica_index].astype(jnp.float32)
        factor = q_init
        for step in range(ITERS):
            image = lax.dot_general(merged, factor, (((1,), (1,)), ((), ())), precision=HIGHEST)
            left_rows = normalize(image)
            factor = lax.dot_general(left_rows, merged, (((0,), (0,)), ((), ())), precision=HIGHEST)
        approx = jnp.dot(left_rows, factor, precision=HIGHEST)
        errors.append((merged - approx).astype(jnp.bfloat16))
        total = total + approx
    update = (total / N_REPLICA).astype(jnp.bfloat16)
    return (update, jnp.stack(errors))
```

```python
import functools

import jax
import jax.numpy as jnp
from jax import lax
from jax.experimental import pallas as pl
from jax.experimental.pallas import tpu as pltpu
from jax.sharding import PartitionSpec as P

F32, BF16 = jnp.float32, jnp.bfloat16
NT = (((1,), (1,)), ((), ()))
MESH = pl.DeviceIdType.MESH


def dot(a, b):
    return jnp.dot(a, b, preferred_element_type=F32)


def dot_nt(a, b, **kw):
    return lax.dot_general(a, b, NT, preferred_element_type=F32, **kw)


def pieces(x):
    hi = x.astype(BF16).astype(F32)
    rest = x - hi
    mid = rest.astype(BF16).astype(F32)
    return jnp.concatenate([hi, mid, rest - mid, jnp.zeros_like(x)], axis=0).astype(BF16)


def fold(x, rank):
    return x[:rank] + x[rank : 2 * rank] + x[2 * rank : 3 * rank]


def inverse_cholesky(gram, rank):
    row = lax.broadcasted_iota(jnp.int32, gram.shape, 0)
    lane = lax.broadcasted_iota(jnp.int32, gram.shape, 1)
    aug = jnp.where(lane < rank, gram, jnp.where(lane == row + rank, 1.0, 0.0))
    for k in range(rank):
        scale = lax.rsqrt(aug[k : k + 1, k : k + 1])
        pivot = aug[k : k + 1, :] * scale
        below = aug - (aug[:, k : k + 1] * scale) * pivot
        aug = jnp.where(row == k, pivot, jnp.where(row > k, below, aug))
    return aug


def apply_inverse(aug, x, rank):
    out = aug[:, rank : rank + 1] * x[0:1]
    for k in range(1, rank):
        out += aug[:, rank + k : rank + k + 1] * x[k : k + 1]
    return out


def kernel(
    n_rep, n_fsdp, side, g_hbm, e_hbm, q_hbm, ne_ref, up_ref,
    g, e, q, img, gram_in, s_out, s_in, f_own, f_all, z_rows, z_fac,
    load_sem, gram_send, gram_recv, s_send, s_recv, f_send, f_recv, zr_send, zr_recv, zf_send, zf_recv,
):
    rank, cols = q.shape
    piece = cols // n_fsdp
    pairs, pair = n_fsdp // 2, 2 * piece
    rep, me = lax.axis_index("replica"), lax.axis_index("fsdp")
    my_y, my_x = me // side, me % side

    barrier = pltpu.get_barrier_semaphore()
    for t in range(1, n_fsdp):
        pl.semaphore_signal(barrier, inc=1, device_id={"fsdp": lax.rem(me + t, n_fsdp)}, device_id_type=MESH)
    for t in range(1, n_rep):
        pl.semaphore_signal(barrier, inc=1, device_id={"replica": lax.rem(rep + t, n_rep)}, device_id_type=MESH)

    loads = [pltpu.make_async_copy(q_hbm, q, load_sem.at[0])]
    for c in range(pairs):
        at = pl.ds(c * pair, pair)
        loads.append(pltpu.make_async_copy(g_hbm.at[0, :, at], g.at[:, at], load_sem.at[1 + 2 * c]))
        loads.append(pltpu.make_async_copy(e_hbm.at[0, :, at], e.at[:, at], load_sem.at[2 + 2 * c]))
    for copy in loads:
        copy.start()

    def others():
        steps = [(dy, dx) for dy in range(side) for dx in range(side) if dy or dx]
        steps.sort(key=lambda s: -(min(s[0], side - s[0]) + min(s[1], side - s[1])))
        return [lax.rem(my_y + dy, side) * side + lax.rem(my_x + dx, side) for dy, dx in steps]

    def to_peer(src, dst, send, recv, peer):
        return pltpu.make_async_remote_copy(
            src_ref=src, dst_ref=dst, send_sem=send, recv_sem=recv, device_id={"fsdp": peer}, device_id_type=MESH
        )

    def gram_copy(it, peer, slot):
        return to_peer(
            gram_in.at[it, me], gram_in.at[it, slot], gram_send.at[it, peer], gram_recv.at[it, slot], peer
        )

    def s_copy(it, peer, slot):
        return to_peer(s_out.at[it, peer], s_in.at[it, slot], s_send.at[it, peer], s_recv.at[it, slot], peer)

    def f_copy(it, peer, slot):
        return to_peer(f_own.at[it], f_all.at[it, slot], f_send.at[it, peer], f_recv.at[it, slot], peer)

    def f_local(it):
        return pltpu.make_async_copy(f_own.at[it], f_all.at[it, me], f_recv.at[it, me])

    def f_pair(it, pp):
        for k in range(2):
            pltpu.make_async_copy(f_own.at[it], f_all.at[it, 2 * pp + k], f_recv.at[it, 2 * pp + k]).wait()
        return jnp.concatenate([f_all[it, 2 * pp], f_all[it, 2 * pp + 1]], axis=1)

    def columns(pp):
        return pl.ds(pl.multiple_of(pp * pair, pair), pair)

    def sweep(it, image):
        wide = jnp.concatenate([image, jnp.zeros((128 - rank, image.shape[1]), F32)], axis=0)
        gram_in[it, me] = dot_nt(image, wide, precision=lax.Precision.HIGHEST)
        for peer in others():
            gram_copy(it, peer, me).start()
        left = pieces(image)
        mine = me // 2
        for t in list(range(1, pairs)) + [0]:
            pp = lax.rem(mine + t, pairs)
            at = columns(pp)
            part = fold(dot(left, g[:, at]) + dot(left, e[:, at]), rank)
            s_out[it, 2 * pp] = part[:, :piece]
            s_out[it, 2 * pp + 1] = part[:, piece:]
            if t:
                s_copy(it, 2 * pp, me).start()
                s_copy(it, 2 * pp + 1, me).start()
            else:
                s_copy(it, me + 1 - 2 * lax.rem(me, 2), me).start()
        for peer in others():
            gram_copy(it, peer, peer).wait_recv()
        gram = gram_in[it, 0]
        for p in range(1, n_fsdp):
            gram += gram_in[it, p]
        inv = inverse_cholesky(gram, rank)
        total = s_out[it, me]
        for peer in others()[::-1]:
            s_copy(it, peer, peer).wait_recv()
            total += s_in[it, peer]
        f_own[it] = apply_inverse(inv, total, rank)
        for peer in others():
            f_copy(it, peer, me).start()
        f_local(it).start()
        return inv

    loads[0].wait()
    image = jnp.zeros((4 * rank, g.shape[0]), F32)
    for c in range(pairs):
        at = pl.ds(c * pair, pair)
        start = pieces(q[:, at])
        loads[1 + 2 * c].wait()
        image += dot_nt(start, g[:, at])
        loads[2 + 2 * c].wait()
        image += dot_nt(start, e[:, at])
    pl.semaphore_wait(barrier, n_fsdp + n_rep - 2)
    sweep(0, fold(image, rank))

    image = jnp.zeros((4 * rank, g.shape[0]), F32)
    mine = me // 2
    for t in range(pairs):
        pp = lax.rem(mine + t, pairs)
        factor = pieces(f_pair(0, pp))
        at = columns(pp)
        image += dot_nt(factor, g[:, at])
        image += dot_nt(factor, e[:, at])
    img[...] = fold(image, rank)
    inv = sweep(1, img[...])

    def to_replica(src, dst, send, recv, peer):
        return pltpu.make_async_remote_copy(
            src_ref=src, dst_ref=dst, send_sem=send, recv_sem=recv, device_id={"replica": peer}, device_id_type=MESH
        )

    def row_copy(peer, slot):
        return to_replica(z_rows.at[rep], z_rows.at[slot], zr_send.at[peer], zr_recv.at[slot], peer)

    def factor_copy(peer, slot):
        return to_replica(
            f_all.at[1, pl.ds(2 * peer, 2)], z_fac.at[slot], zf_send.at[peer], zf_recv.at[slot], peer
        )

    rows_t = apply_inverse(inv, img[...], rank)
    z_rows[rep] = rows_t
    replicas = [lax.rem(rep + t, n_rep) for t in range(1, n_rep)]
    for peer in replicas:
        row_copy(peer, rep).start()

    def halves(x):
        hi = x.astype(BF16).astype(F32)
        return hi, x - hi

    hi, mid = halves(rows_t)
    left = jnp.concatenate([hi, hi, mid, mid], axis=0).T.astype(BF16)
    for t in list(range(1, n_rep)) + [0]:
        pp = lax.rem(rep + t, n_rep)
        factor = f_pair(1, pp)
        if t:
            factor_copy(pp, rep).start()
        else:
            z_fac[rep] = f_all[1, pl.ds(2 * rep, 2)]
        hi, mid = halves(factor)
        right = jnp.concatenate([hi, mid, hi, mid], axis=0).astype(BF16)
        at = columns(pp)
        ne_ref[0, :, at] = (g[:, at].astype(F32) + e[:, at].astype(F32) - dot(left, right)).astype(BF16)

    for peer in replicas:
        row_copy(peer, peer).wait_recv()
        factor_copy(peer, peer).wait_recv()
    hi, mid = halves(z_rows[...].reshape(n_rep * rank, -1))
    left = jnp.concatenate([hi, hi, mid], axis=0).T.astype(BF16)
    for k in range(2):
        hi, mid = halves(z_fac[:, k].reshape(n_rep * rank, piece))
        right = jnp.concatenate([hi, mid, hi], axis=0).astype(BF16)
        up_ref[:, k * piece : (k + 1) * piece] = (dot(left, right) * (1.0 / n_rep)).astype(BF16)

    for it in range(2):
        for peer in others():
            gram_copy(it, peer, me).wait_send()
            s_copy(it, peer, me).wait_send()
            f_copy(it, peer, me).wait_send()
    for peer in replicas:
        row_copy(peer, rep).wait_send()
        factor_copy(peer, rep).wait_send()


def shards(n_rep, n_fsdp, outer_grad, error_prev, q_init):
    rank, cols = q_init.shape
    rows = outer_grad.shape[1]
    piece = cols // n_fsdp
    side = 4
    dma = pltpu.SemaphoreType.DMA
    update, new_error = None, None
    new_error, update = pl.pallas_call(
        functools.partial(kernel, n_rep, n_fsdp, side),
        out_shape=OUT((1, rows, cols), (rows, cols // n_rep)),
        in_specs=[pl.BlockSpec(memory_space=pl.ANY)] * 3,
        out_specs=OUT_SPECS,
        scratch_shapes=[
            pltpu.VMEM((rows, cols), BF16),
            pltpu.VMEM((rows, cols), BF16),
            pltpu.VMEM((rank, cols), F32),
            pltpu.VMEM((rank, rows), F32),
            pltpu.VMEM((2, n_fsdp, rank, 128), F32),
            pltpu.VMEM((2, n_fsdp, rank, piece), F32),
            pltpu.VMEM((2, n_fsdp, rank, piece), F32),
            pltpu.VMEM((2, rank, piece), F32),
            pltpu.VMEM((2, n_fsdp, rank, piece), F32),
            pltpu.VMEM((n_rep, rank, rows), F32),
            pltpu.VMEM((n_rep, 2, rank, piece), F32),
            dma((1 + n_fsdp,)),
            dma((2, n_fsdp)),
            dma((2, n_fsdp)),
            dma((2, n_fsdp)),
            dma((2, n_fsdp)),
            dma((2, n_fsdp)),
            dma((2, n_fsdp)),
            dma((n_rep,)),
            dma((n_rep,)),
            dma((n_rep,)),
            dma((n_rep,)),
        ],
        compiler_params=pltpu.CompilerParams(
            collective_id=0, has_side_effects=True, vmem_limit_bytes=VMEM_LIMIT
        ),
    )(outer_grad, error_prev, q_init)
    return update, new_error


VMEM_LIMIT = 40 << 20
OUT_SPECS = [pl.BlockSpec(memory_space=pltpu.VMEM)] * 2


def OUT(a, b):
    return [pltpu.VMEM(a, BF16), pltpu.VMEM(b, BF16)]


def solution(mesh):
    n_rep, n_fsdp = mesh.shape["replica"], mesh.shape["fsdp"]
    return jax.shard_map(
        functools.partial(shards, n_rep, n_fsdp),
        mesh=mesh,
        in_specs=(P("replica", "fsdp", None), P("replica", "fsdp", None), P()),
        out_specs=(P("fsdp", "replica"), P("replica", "fsdp", None)),
        check_vma=False,
    )
```

```python
import functools
import math

import jax
import jax.numpy as jnp
from jax import lax
from jax.experimental import pallas as pl
from jax.experimental.pallas import tpu as pltpu
from jax.sharding import PartitionSpec as P

F32, BF16 = jnp.float32, jnp.bfloat16
NT = (((1,), (1,)), ((), ()))
MESH = pl.DeviceIdType.MESH


def dot(a, b):
    return jnp.dot(a, b, preferred_element_type=F32)


def dot_nt(a, b, **kw):
    return lax.dot_general(a, b, NT, preferred_element_type=F32, **kw)


def pieces(x):
    hi = x.astype(BF16).astype(F32)
    rest = x - hi
    mid = rest.astype(BF16).astype(F32)
    return jnp.concatenate([hi, mid, rest - mid, jnp.zeros_like(x)], axis=0).astype(BF16)


def fold(x, rank):
    return x[:rank] + x[rank : 2 * rank] + x[2 * rank : 3 * rank]


def inverse_cholesky(gram, rank):
    row = lax.broadcasted_iota(jnp.int32, gram.shape, 0)
    lane = lax.broadcasted_iota(jnp.int32, gram.shape, 1)

    def step(k, aug):
        top = jnp.sum(jnp.where(row == k, aug, 0.0), axis=0, keepdims=True)
        side = jnp.sum(jnp.where(lane == k, aug, 0.0), axis=1, keepdims=True)
        scale = lax.rsqrt(jnp.sum(jnp.where(row == k, side, 0.0), axis=0, keepdims=True))
        pivot = top * scale
        return jnp.where(row == k, pivot, jnp.where(row > k, aug - (side * scale) * pivot, aug))

    aug = jnp.where(lane < rank, gram, jnp.where(lane == row + rank, 1.0, 0.0))
    return lax.fori_loop(0, rank, step, aug)


def apply_inverse(aug, x, rank):
    out = aug[:, rank : rank + 1] * x[0:1]
    for k in range(1, rank):
        out += aug[:, rank + k : rank + k + 1] * x[k : k + 1]
    return out


def halves(x):
    hi = x.astype(BF16).astype(F32)
    return hi, x - hi


def kernel(
    n_rep, n_fsdp, side, g_hbm, e_hbm, q_hbm, ne_ref, z_rows, z_fac,
    g, e, q, img, inv, gram_in, s_out, s_in, f_own, f_all,
    load_sem, gram_send, gram_recv, s_send, s_recv, f_send, f_recv, zr_send, zr_recv, zf_send, zf_recv,
):
    rank, cols = q.shape
    piece = cols // n_fsdp
    pairs, pair = n_fsdp // 2, 2 * piece
    rep, me = lax.axis_index("replica"), lax.axis_index("fsdp")
    my_y, my_x = me // side, me % side

    def columns(pp):
        return pl.ds(pl.multiple_of(pp * pair, pair), pair)

    def loads(c):
        at = columns(c)
        return (
            pltpu.make_async_copy(g_hbm.at[0, :, at], g.at[:, at], load_sem.at[2 * c]),
            pltpu.make_async_copy(e_hbm.at[0, :, at], e.at[:, at], load_sem.at[2 * c + 1]),
        )

    load_q = pltpu.make_async_copy(q_hbm, q, load_sem.at[2 * pairs])
    load_q.start()
    for c in range(pairs):
        for copy in loads(c):
            copy.start()

    barrier = pltpu.get_barrier_semaphore()
    for t in range(1, n_fsdp):
        pl.semaphore_signal(barrier, inc=1, device_id={"fsdp": lax.rem(me + t, n_fsdp)}, device_id_type=MESH)
    for t in range(1, n_rep):
        pl.semaphore_signal(barrier, inc=1, device_id={"replica": lax.rem(rep + t, n_rep)}, device_id_type=MESH)

    def far(step, size):
        return min(step, size - step)

    def others():
        steps = [(dy, dx) for dy in range(side) for dx in range(side) if dy or dx]
        steps.sort(key=lambda s: far(s[0], side) + far(s[1], side))
        return [lax.rem(my_y + dy, side) * side + lax.rem(my_x + dx, side) for dy, dx in steps]

    def near_pair(t):
        half = side // 2
        u = t // half
        dy = (u + 1) // 2 * (2 * (u % 2) - 1) + side
        return lax.rem(my_y + dy, side) * half + lax.rem(my_x // 2 + t, half)

    def to_peer(src, dst, send, recv, peer):
        return pltpu.make_async_remote_copy(
            src_ref=src, dst_ref=dst, send_sem=send, recv_sem=recv, device_id={"fsdp": peer}, device_id_type=MESH
        )

    def gram_copy(it, peer):
        return to_peer(gram_in.at[it, me], gram_in.at[it, me], gram_send.at[it], gram_recv.at[it], peer)

    def s_copy(it, peer):
        return to_peer(s_out.at[it, peer], s_in.at[it, me], s_send.at[it], s_recv.at[it], peer)

    def f_copy(it, peer):
        return to_peer(f_own.at[it], f_all.at[it, me], f_send.at[it], f_recv.at[it, me // 2], peer)

    def f_local(it):
        return pltpu.make_async_copy(f_own.at[it], f_all.at[it, me], f_recv.at[it, me // 2])

    def from_others(buffer, sem):
        part = buffer.at[pl.ds(0, buffer.shape[0] - 1)]
        return pltpu.make_async_copy(part, part, sem)

    def f_pair(it, pp):
        both = f_all.at[it, pl.ds(2 * pp, 2)]
        pltpu.make_async_copy(both, both, f_recv.at[it, pp]).wait()
        return jnp.concatenate([f_all[it, 2 * pp], f_all[it, 2 * pp + 1]], axis=1)

    def sweep(it):
        image = img[...]
        left = pieces(image)

        def part_of_factor(t, carry):
            pp = near_pair(pairs - 1 - t)
            at = columns(pp)
            part = fold(dot(left, g[:, at]) + dot(left, e[:, at]), rank)
            s_out[it, 2 * pp] = part[:, :piece]
            s_out[it, 2 * pp + 1] = part[:, piece:]
            for k in range(2):

                @pl.when(2 * pp + k != me)
                def _():
                    s_copy(it, 2 * pp + k).start()

            @pl.when(t == 1)
            def _():
                wide = jnp.concatenate([image, jnp.zeros((128 - rank, image.shape[1]), F32)], axis=0)
                gram_in[it, me] = dot_nt(image, wide, precision=lax.Precision.HIGHEST)
                for peer in others()[::-1]:
                    gram_copy(it, peer).start()

            return carry

        lax.fori_loop(0, pairs, part_of_factor, 0)
        from_others(gram_in.at[it], gram_recv.at[it]).wait()
        gram = gram_in[it, 0]
        for p in range(1, n_fsdp):
            gram += gram_in[it, p]
        inv[...] = inverse_cholesky(gram, rank)
        from_others(s_in.at[it], s_recv.at[it]).wait()
        total = s_out[it, me]
        for peer in others():
            total += s_in[it, peer]
        f_own[it] = apply_inverse(inv[...], total, rank)
        for peer in others():
            f_copy(it, peer).start()
        f_local(it).start()

    load_q.wait()

    def first_image(c, image):
        for copy in loads(c):
            copy.wait()
        at = columns(c)
        start = pieces(q[:, at])
        return image + dot_nt(start, g[:, at]) + dot_nt(start, e[:, at])

    zero = jnp.zeros((4 * rank, g.shape[0]), F32)
    img[...] = fold(lax.fori_loop(0, pairs, first_image, zero), rank)
    pl.semaphore_wait(barrier, n_fsdp + n_rep - 2)
    sweep(0)

    def second_image(t, image):
        pp = near_pair(t)
        factor = pieces(f_pair(0, pp))
        at = columns(pp)
        return image + dot_nt(factor, g[:, at]) + dot_nt(factor, e[:, at])

    img[...] = fold(lax.fori_loop(0, pairs, second_image, zero), rank)
    sweep(1)

    def to_replica(src, dst, send, recv, peer):
        return pltpu.make_async_remote_copy(
            src_ref=src, dst_ref=dst, send_sem=send, recv_sem=recv, device_id={"replica": peer}, device_id_type=MESH
        )

    def row_copy(peer):
        return to_replica(z_rows.at[rep], z_rows.at[rep], zr_send, zr_recv, peer)

    def factor_copy(peer):
        return to_replica(f_all.at[1, pl.ds(2 * peer, 2)], z_fac.at[rep], zf_send, zf_recv, peer)

    rows_t = apply_inverse(inv[...], img[...], rank)
    z_rows[rep] = rows_t
    for t in range(1, n_rep):
        row_copy(lax.rem(rep + t, n_rep)).start()
    hi, mid = halves(rows_t)
    left = jnp.concatenate([hi, hi, mid, mid], axis=0).T.astype(BF16)

    def error(t, carry):
        pp = near_pair(t)
        factor = f_pair(1, pp)

        @pl.when(pp != rep)
        def _():
            factor_copy(pp).start()

        hi, mid = halves(factor)
        right = jnp.concatenate([hi, mid, hi, mid], axis=0).astype(BF16)
        at = columns(pp)
        ne_ref[0, :, at] = (g[:, at].astype(F32) + e[:, at].astype(F32) - dot(left, right)).astype(BF16)
        return carry

    lax.fori_loop(0, pairs, error, 0)
    z_fac[rep] = f_all[1, pl.ds(2 * rep, 2)]
    from_others(z_rows, zr_recv).wait()
    from_others(z_fac, zf_recv).wait()

    for it in range(2):
        from_others(gram_in.at[it], gram_send.at[it]).wait()
        from_others(s_out.at[it], s_send.at[it]).wait()
        from_others(f_all.at[it], f_send.at[it]).wait()
    from_others(z_rows, zr_send).wait()
    from_others(z_fac, zf_send).wait()


def finish(ne, z_rows, z_fac, ne_hbm, up_hbm, up, sems):
    n_rep, rank, rows = z_rows.shape
    piece = z_fac.shape[3]
    blocks = sems.shape[0] - 1
    height = rows // blocks
    copies = []
    for b in range(blocks):
        at = pl.ds(b * height, height)
        copies.append(pltpu.make_async_copy(ne.at[0, at], ne_hbm.at[0, at], sems.at[b]))
        copies[-1].start()
    hi, mid = halves(z_rows[...].reshape(n_rep * rank, rows))
    left = jnp.concatenate([hi, hi, mid], axis=0).T.astype(BF16)
    for k in range(2):
        hi, mid = halves(z_fac[:, k].reshape(n_rep * rank, piece))
        right = jnp.concatenate([hi, mid, hi], axis=0).astype(BF16)
        up[:, k * piece : (k + 1) * piece] = (dot(left, right) * (1.0 / n_rep)).astype(BF16)
    copies.append(pltpu.make_async_copy(up, up_hbm, sems.at[blocks]))
    copies[-1].start()
    for copy in copies:
        copy.wait()


def shards(n_rep, n_fsdp, outer_grad, error_prev, q_init):
    rank, cols = q_init.shape
    rows = outer_grad.shape[1]
    piece = cols // n_fsdp
    side = math.isqrt(n_fsdp)
    dma = pltpu.SemaphoreType.DMA
    vmem = pl.BlockSpec(memory_space=pltpu.VMEM)
    hbm = pl.BlockSpec(memory_space=pltpu.HBM)
    parts = pl.pallas_call(
        functools.partial(kernel, n_rep, n_fsdp, side),
        out_shape=[
            pltpu.VMEM((1, rows, cols), BF16),
            pltpu.VMEM((n_rep, rank, rows), F32),
            pltpu.VMEM((n_rep, 2, rank, piece), F32),
        ],
        in_specs=[hbm] * 3,
        out_specs=[vmem] * 3,
        scratch_shapes=[
            pltpu.VMEM((rows, cols), BF16),
            pltpu.VMEM((rows, cols), BF16),
            pltpu.VMEM((rank, cols), F32),
            pltpu.VMEM((rank, rows), F32),
            pltpu.VMEM((rank, 128), F32),
            pltpu.VMEM((2, n_fsdp, rank, 128), F32),
            pltpu.VMEM((2, n_fsdp, rank, piece), F32),
            pltpu.VMEM((2, n_fsdp, rank, piece), F32),
            pltpu.VMEM((2, rank, piece), F32),
            pltpu.VMEM((2, n_fsdp, rank, piece), F32),
            dma((1 + n_fsdp,)),
            dma((2,)),
            dma((2,)),
            dma((2,)),
            dma((2,)),
            dma((2,)),
            dma((2, n_fsdp // 2)),
            dma,
            dma,
            dma,
            dma,
        ],
        compiler_params=pltpu.CompilerParams(
            collective_id=0, has_side_effects=True, vmem_limit_bytes=VMEM_LIMIT
        ),
    )(*(pltpu.with_memory_space_constraint(x, pltpu.HBM) for x in (outer_grad, error_prev, q_init)))
    new_error, update = pl.pallas_call(
        finish,
        out_shape=[pltpu.HBM((1, rows, cols), BF16), pltpu.HBM((rows, cols // n_rep), BF16)],
        in_specs=[vmem] * 3,
        out_specs=[hbm] * 2,
        scratch_shapes=[pltpu.VMEM((rows, cols // n_rep), BF16), dma((9,))],
        compiler_params=pltpu.CompilerParams(vmem_limit_bytes=16 << 20),
    )(*(pltpu.with_memory_space_constraint(x, pltpu.VMEM) for x in parts))
    return update, new_error


VMEM_LIMIT = 40 << 20


def solution(mesh):
    n_rep, n_fsdp = mesh.shape["replica"], mesh.shape["fsdp"]
    return jax.shard_map(
        functools.partial(shards, n_rep, n_fsdp),
        mesh=mesh,
        in_specs=(P("replica", "fsdp", None), P("replica", "fsdp", None), P()),
        out_specs=(P("fsdp", "replica"), P("replica", "fsdp", None)),
        check_vma=False,
    )
```

```python
import functools
import math

import jax
import jax.numpy as jnp
from jax import lax
from jax.experimental import pallas as pl
from jax.experimental.pallas import tpu as pltpu
from jax.sharding import PartitionSpec as P

F32, BF16 = jnp.float32, jnp.bfloat16
NT = (((1,), (1,)), ((), ()))
MESH = pl.DeviceIdType.MESH


def dot(a, b):
    return jnp.dot(a, b, preferred_element_type=F32)


def dot_nt(a, b, **kw):
    return lax.dot_general(a, b, NT, preferred_element_type=F32, **kw)


def pieces(x):
    hi = x.astype(BF16).astype(F32)
    rest = x - hi
    mid = rest.astype(BF16).astype(F32)
    return jnp.concatenate([hi, mid, rest - mid, jnp.zeros_like(x)], axis=0).astype(BF16)


def fold(x, rank):
    return x[:rank] + x[rank : 2 * rank] + x[2 * rank : 3 * rank]


def inverse_cholesky(gram, rank):
    row = lax.broadcasted_iota(jnp.int32, gram.shape, 0)
    lane = lax.broadcasted_iota(jnp.int32, gram.shape, 1)

    def step(k, aug):
        top = jnp.sum(jnp.where(row == k, aug, 0.0), axis=0, keepdims=True)
        side = jnp.sum(jnp.where(lane == k, aug, 0.0), axis=1, keepdims=True)
        scale = lax.rsqrt(jnp.sum(jnp.where(row == k, side, 0.0), axis=0, keepdims=True))
        pivot = top * scale
        return jnp.where(row == k, pivot, jnp.where(row > k, aug - (side * scale) * pivot, aug))

    aug = jnp.where(lane < rank, gram, jnp.where(lane == row + rank, 1.0, 0.0))
    return lax.fori_loop(0, rank, step, aug)


def apply_inverse(aug, x, rank):
    out = aug[:, rank : rank + 1] * x[0:1]
    for k in range(1, rank):
        out += aug[:, rank + k : rank + k + 1] * x[k : k + 1]
    return out


def halves(x):
    hi = x.astype(BF16).astype(F32)
    return hi, x - hi


def kernel(
    n_rep, n_fsdp, side, g_hbm, e_hbm, q_hbm, ne_ref, z_rows, z_fac,
    g, e, g_t, e_t, q, img, inv, gram_in, s_out, s_in, f_own, f_all,
    load_sem, gram_send, gram_recv, s_send, s_recv, f_send, f_recv, zr_send, zr_recv, zf_send, zf_recv,
):
    rank, cols = q.shape
    piece = cols // n_fsdp
    pairs, pair = n_fsdp // 2, 2 * piece
    rep, me = lax.axis_index("replica"), lax.axis_index("fsdp")
    my_y, my_x = me // side, me % side

    def columns(pp):
        return pl.ds(pl.multiple_of(pp * pair, pair), pair)

    def loads(c):
        at = columns(c)
        return (
            pltpu.make_async_copy(g_hbm.at[0, :, at], g.at[:, at], load_sem.at[2 * c]),
            pltpu.make_async_copy(e_hbm.at[0, :, at], e.at[:, at], load_sem.at[2 * c + 1]),
        )

    load_q = pltpu.make_async_copy(q_hbm, q, load_sem.at[2 * pairs])
    load_q.start()
    for c in range(pairs):
        for copy in loads(c):
            copy.start()

    barrier = pltpu.get_barrier_semaphore()
    for t in range(1, n_fsdp):
        pl.semaphore_signal(barrier, inc=1, device_id={"fsdp": lax.rem(me + t, n_fsdp)}, device_id_type=MESH)
    for t in range(1, n_rep):
        pl.semaphore_signal(barrier, inc=1, device_id={"replica": lax.rem(rep + t, n_rep)}, device_id_type=MESH)

    def far(step, size):
        return min(step, size - step)

    def others():
        steps = [(dy, dx) for dy in range(side) for dx in range(side) if dy or dx]
        steps.sort(key=lambda s: far(s[0], side) + far(s[1], side))
        return [lax.rem(my_y + dy, side) * side + lax.rem(my_x + dx, side) for dy, dx in steps]

    def near_pair(t):
        half = side // 2
        u = t // half
        dy = (u + 1) // 2 * (2 * (u % 2) - 1) + side
        return lax.rem(my_y + dy, side) * half + lax.rem(my_x // 2 + t, half)

    def to_peer(src, dst, send, recv, peer):
        return pltpu.make_async_remote_copy(
            src_ref=src, dst_ref=dst, send_sem=send, recv_sem=recv, device_id={"fsdp": peer}, device_id_type=MESH
        )

    def gram_copy(it, peer):
        return to_peer(gram_in.at[it, me], gram_in.at[it, me], gram_send.at[it], gram_recv.at[it], peer)

    def s_copy(it, peer):
        return to_peer(s_out.at[it, peer], s_in.at[it, me], s_send.at[it], s_recv.at[it], peer)

    def f_copy(it, peer):
        return to_peer(f_own.at[it], f_all.at[it, me], f_send.at[it], f_recv.at[it, me // 2], peer)

    def f_local(it):
        return pltpu.make_async_copy(f_own.at[it], f_all.at[it, me], f_recv.at[it, me // 2])

    def from_others(buffer, sem):
        part = buffer.at[pl.ds(0, buffer.shape[0] - 1)]
        return pltpu.make_async_copy(part, part, sem)

    def f_pair(it, pp):
        both = f_all.at[it, pl.ds(2 * pp, 2)]
        pltpu.make_async_copy(both, both, f_recv.at[it, pp]).wait()
        return jnp.concatenate([f_all[it, 2 * pp], f_all[it, 2 * pp + 1]], axis=1)

    def sweep(it):
        image = img[...]
        left = pieces(image)

        def row_at(t):
            dy = side - 1 - t
            return lax.rem(my_y + (dy + 1) // 2 * (2 * (dy % 2) - 1) + side, side)

        def row_of_factor(t):
            first = row_at(t) * side
            for k in range(side):
                at = pl.ds(pl.multiple_of((first + k) * piece, piece), piece)
                s_out[it, first + k] = fold(dot(left, g[:, at]) + dot(left, e[:, at]), rank)

        def send_row(t):
            for dx in range(side):
                s_copy(it, row_at(t) * side + lax.rem(my_x + 2 + dx, side)).start()

        def next_row(t, carry):
            send_row(t - 1)
            row_of_factor(t)
            return carry

        row_of_factor(0)
        wide = jnp.concatenate([left, jnp.zeros((96, left.shape[1]), BF16)], axis=0)
        terms = fold(dot_nt(left, wide), rank)
        gram_in[it, me] = terms + pltpu.roll(terms, 128 - rank, 1) + pltpu.roll(terms, 128 - 2 * rank, 1)
        lax.fori_loop(1, side, next_row, 0)
        for dx in range(1, side):
            s_copy(it, my_y * side + lax.rem(my_x + dx, side)).start()
        for peer in others()[::-1]:
            gram_copy(it, peer).start()
        from_others(s_in.at[it], s_recv.at[it]).wait()
        total = s_out[it, me]
        for peer in others():
            total += s_in[it, peer]
        f_own[it] = total
        for peer in others():
            f_copy(it, peer).start()
        f_local(it).start()
        from_others(gram_in.at[it], gram_recv.at[it]).wait()
        gram = gram_in[it, 0]
        for p in range(1, n_fsdp):
            gram += gram_in[it, p]
        inv[...] = inverse_cholesky(gram, rank)

    load_q.wait()

    def first_image(c, image):
        for copy in loads(c):
            copy.wait()
        at = columns(c)
        start = pieces(q[:, at])
        g_t[at, :] = g[:, at].T
        e_t[at, :] = e[:, at].T
        return image + dot(start, g_t[at, :]) + dot(start, e_t[at, :])

    zero = jnp.zeros((4 * rank, g.shape[0]), F32)
    img[...] = fold(lax.fori_loop(0, pairs, first_image, zero), rank)
    pl.semaphore_wait(barrier, n_fsdp + n_rep - 2)
    sweep(0)

    def second_image(t, image):
        pp = near_pair(t)
        factor = pieces(apply_inverse(inv[...], f_pair(0, pp), rank))
        at = columns(pp)
        return image + dot(factor, g_t[at, :]) + dot(factor, e_t[at, :])

    img[...] = fold(lax.fori_loop(0, pairs, second_image, zero), rank)
    sweep(1)

    def to_replica(src, dst, send, recv, peer):
        return pltpu.make_async_remote_copy(
            src_ref=src, dst_ref=dst, send_sem=send, recv_sem=recv, device_id={"replica": peer}, device_id_type=MESH
        )

    def row_copy(peer):
        return to_replica(z_rows.at[rep], z_rows.at[rep], zr_send, zr_recv, peer)

    def factor_copy(peer):
        return to_replica(f_all.at[1, pl.ds(2 * peer, 2)], z_fac.at[rep], zf_send, zf_recv, peer)

    rows_t = apply_inverse(inv[...], img[...], rank)
    z_rows[rep] = rows_t
    for t in range(1, n_rep):
        row_copy(lax.rem(rep + t, n_rep)).start()
    hi, mid = halves(rows_t)
    left = jnp.concatenate([hi, hi, mid, mid], axis=0).T.astype(BF16)

    def forward(t, carry):
        pp = near_pair(t)
        factor = apply_inverse(inv[...], f_pair(1, pp), rank)
        f_all[1, 2 * pp] = factor[:, :piece]
        f_all[1, 2 * pp + 1] = factor[:, piece:]

        @pl.when(pp != rep)
        def _():
            factor_copy(pp).start()

        return carry

    def error(t, carry):
        pp = near_pair(t)
        hi, mid = halves(jnp.concatenate([f_all[1, 2 * pp], f_all[1, 2 * pp + 1]], axis=1))
        right = jnp.concatenate([hi, mid, hi, mid], axis=0).astype(BF16)
        at = columns(pp)
        ne_ref[0, :, at] = (g[:, at].astype(F32) + e[:, at].astype(F32) - dot(left, right)).astype(BF16)
        return carry

    lax.fori_loop(0, pairs, forward, 0)
    lax.fori_loop(0, pairs, error, 0)
    z_fac[rep] = f_all[1, pl.ds(2 * rep, 2)]
    from_others(z_rows, zr_recv).wait()
    from_others(z_fac, zf_recv).wait()

    for it in range(2):
        from_others(gram_in.at[it], gram_send.at[it]).wait()
        from_others(s_out.at[it], s_send.at[it]).wait()
        from_others(f_all.at[it], f_send.at[it]).wait()
    from_others(z_rows, zr_send).wait()
    from_others(z_fac, zf_send).wait()


def finish(ne, z_rows, z_fac, ne_hbm, up_hbm, up, sems):
    n_rep, rank, rows = z_rows.shape
    piece = z_fac.shape[3]
    blocks = sems.shape[0] - 1
    height = rows // blocks
    copies = []
    for b in range(blocks):
        at = pl.ds(b * height, height)
        copies.append(pltpu.make_async_copy(ne.at[0, at], ne_hbm.at[0, at], sems.at[b]))
        copies[-1].start()
    hi, mid = halves(z_rows[...].reshape(n_rep * rank, rows))
    left = jnp.concatenate([hi, hi, mid], axis=0).T.astype(BF16)
    for k in range(2):
        hi, mid = halves(z_fac[:, k].reshape(n_rep * rank, piece))
        right = jnp.concatenate([hi, mid, hi], axis=0).astype(BF16)
        up[:, k * piece : (k + 1) * piece] = (dot(left, right) * (1.0 / n_rep)).astype(BF16)
    copies.append(pltpu.make_async_copy(up, up_hbm, sems.at[blocks]))
    copies[-1].start()
    for copy in copies:
        copy.wait()


def shards(n_rep, n_fsdp, outer_grad, error_prev, q_init):
    rank, cols = q_init.shape
    rows = outer_grad.shape[1]
    piece = cols // n_fsdp
    side = math.isqrt(n_fsdp)
    dma = pltpu.SemaphoreType.DMA
    vmem = pl.BlockSpec(memory_space=pltpu.VMEM)
    hbm = pl.BlockSpec(memory_space=pltpu.HBM)
    parts = pl.pallas_call(
        functools.partial(kernel, n_rep, n_fsdp, side),
        out_shape=[
            pltpu.VMEM((1, rows, cols), BF16),
            pltpu.VMEM((n_rep, rank, rows), F32),
            pltpu.VMEM((n_rep, 2, rank, piece), F32),
        ],
        in_specs=[hbm] * 3,
        out_specs=[vmem] * 3,
        scratch_shapes=[
            pltpu.VMEM((rows, cols), BF16),
            pltpu.VMEM((rows, cols), BF16),
            pltpu.VMEM((cols, rows), BF16),
            pltpu.VMEM((cols, rows), BF16),
            pltpu.VMEM((rank, cols), F32),
            pltpu.VMEM((rank, rows), F32),
            pltpu.VMEM((rank, 128), F32),
            pltpu.VMEM((2, n_fsdp, rank, 128), F32),
            pltpu.VMEM((2, n_fsdp, rank, piece), F32),
            pltpu.VMEM((2, n_fsdp, rank, piece), F32),
            pltpu.VMEM((2, rank, piece), F32),
            pltpu.VMEM((2, n_fsdp, rank, piece), F32),
            dma((1 + n_fsdp,)),
            dma((2,)),
            dma((2,)),
            dma((2,)),
            dma((2,)),
            dma((2,)),
            dma((2, n_fsdp // 2)),
            dma,
            dma,
            dma,
            dma,
        ],
        compiler_params=pltpu.CompilerParams(
            collective_id=0, has_side_effects=True, vmem_limit_bytes=VMEM_LIMIT
        ),
    )(*(pltpu.with_memory_space_constraint(x, pltpu.HBM) for x in (outer_grad, error_prev, q_init)))
    new_error, update = pl.pallas_call(
        finish,
        out_shape=[pltpu.HBM((1, rows, cols), BF16), pltpu.HBM((rows, cols // n_rep), BF16)],
        in_specs=[vmem] * 3,
        out_specs=[hbm] * 2,
        scratch_shapes=[pltpu.VMEM((rows, cols // n_rep), BF16), dma((9,))],
        compiler_params=pltpu.CompilerParams(vmem_limit_bytes=16 << 20),
    )(*(pltpu.with_memory_space_constraint(x, pltpu.VMEM) for x in parts))
    return update, new_error


VMEM_LIMIT = 46 << 20


def solution(mesh):
    n_rep, n_fsdp = mesh.shape["replica"], mesh.shape["fsdp"]
    return jax.shard_map(
        functools.partial(shards, n_rep, n_fsdp),
        mesh=mesh,
        in_specs=(P("replica", "fsdp", None), P("replica", "fsdp", None), P()),
        out_specs=(P("fsdp", "replica"), P("replica", "fsdp", None)),
        check_vma=False,
    )
```

```python
import functools
import math

import jax
import jax.numpy as jnp
from jax import lax
from jax.experimental import pallas as pl
from jax.experimental.pallas import tpu as pltpu
from jax.sharding import PartitionSpec as P

F32, BF16 = jnp.float32, jnp.bfloat16
NT = (((1,), (1,)), ((), ()))
MESH = pl.DeviceIdType.MESH


def dot(a, b):
    return jnp.dot(a, b, preferred_element_type=F32)


def dot_nt(a, b, **kw):
    return lax.dot_general(a, b, NT, preferred_element_type=F32, **kw)


def pieces(x):
    hi = x.astype(BF16).astype(F32)
    rest = x - hi
    mid = rest.astype(BF16).astype(F32)
    return jnp.concatenate([hi, mid, rest - mid, jnp.zeros_like(x)], axis=0).astype(BF16)


def fold(x, rank):
    return x[:rank] + x[rank : 2 * rank] + x[2 * rank : 3 * rank]


def inverse_cholesky(gram, rank):
    row = lax.broadcasted_iota(jnp.int32, gram.shape, 0)
    lane = lax.broadcasted_iota(jnp.int32, gram.shape, 1)

    def step(k, aug):
        top = jnp.sum(jnp.where(row == k, aug, 0.0), axis=0, keepdims=True)
        side = jnp.sum(jnp.where(lane == k, aug, 0.0), axis=1, keepdims=True)
        scale = lax.rsqrt(jnp.sum(jnp.where(row == k, side, 0.0), axis=0, keepdims=True))
        pivot = top * scale
        return jnp.where(row == k, pivot, jnp.where(row > k, aug - (side * scale) * pivot, aug))

    aug = jnp.where(lane < rank, gram, jnp.where(lane == row + rank, 1.0, 0.0))
    return lax.fori_loop(0, rank, step, aug)


def apply_inverse(aug, x, rank):
    out = aug[:, rank : rank + 1] * x[0:1]
    for k in range(1, rank):
        out += aug[:, rank + k : rank + k + 1] * x[k : k + 1]
    return out


def halves(x):
    hi = x.astype(BF16).astype(F32)
    return hi, x - hi


def kernel(
    n_rep, n_fsdp, side, g_hbm, e_hbm, q_hbm, ne_ref, z_rows, z_fac,
    g, e, g_t, e_t, q, img, inv, gram_in, s_out, s_in, f_own, f_all,
    load_sem, gram_send, gram_recv, s_send, s_recv, f_send, f_recv, zr_send, zr_recv, zf_send, zf_recv,
):
    rank, cols = q.shape
    piece = cols // n_fsdp
    pairs, pair = n_fsdp // 2, 2 * piece
    rep, me = lax.axis_index("replica"), lax.axis_index("fsdp")
    my_y, my_x = me // side, me % side

    def columns(pp):
        return pl.ds(pl.multiple_of(pp * pair, pair), pair)

    def loads(c):
        at = columns(c)
        return (
            pltpu.make_async_copy(g_hbm.at[0, :, at], g.at[:, at], load_sem.at[2 * c]),
            pltpu.make_async_copy(e_hbm.at[0, :, at], e.at[:, at], load_sem.at[2 * c + 1]),
        )

    load_q = pltpu.make_async_copy(q_hbm, q, load_sem.at[2 * pairs])
    load_q.start()
    for c in range(pairs):
        for copy in loads(c):
            copy.start()

    barrier = pltpu.get_barrier_semaphore()
    for t in range(1, n_fsdp):
        pl.semaphore_signal(barrier, inc=1, device_id={"fsdp": lax.rem(me + t, n_fsdp)}, device_id_type=MESH)
    for t in range(1, n_rep):
        pl.semaphore_signal(barrier, inc=1, device_id={"replica": lax.rem(rep + t, n_rep)}, device_id_type=MESH)

    def far(step, size):
        return min(step, size - step)

    def others():
        steps = [(dy, dx) for dy in range(side) for dx in range(side) if dy or dx]
        steps.sort(key=lambda s: (far(s[0], side), far(s[1], side)))
        return [lax.rem(my_y + dy, side) * side + lax.rem(my_x + dx, side) for dy, dx in steps]

    def over_pairs(step, carry):
        half = side // 2

        def run(rows, count, carry):
            def at(j, carry):
                row = lax.rem(my_y + rows(lax.rem(j, count)) + side, side)
                return step(row * half + lax.rem(my_x // 2 + j // count, half), carry)

            return lax.fori_loop(0, count * half, at, carry)

        carry = run(lambda j: 0 * j, 1, carry)
        carry = run(lambda j: 1 - 2 * j, 2, carry)
        return run(lambda j: 2 + j, side - 3, carry)

    def to_peer(src, dst, send, recv, peer):
        return pltpu.make_async_remote_copy(
            src_ref=src, dst_ref=dst, send_sem=send, recv_sem=recv, device_id={"fsdp": peer}, device_id_type=MESH
        )

    def gram_copy(it, peer):
        return to_peer(gram_in.at[it, me], gram_in.at[it, me], gram_send.at[it], gram_recv.at[it], peer)

    def s_copy(it, peer):
        return to_peer(s_out.at[it, peer], s_in.at[it, me], s_send.at[it], s_recv.at[it], peer)

    def f_copy(it, peer):
        return to_peer(f_own.at[it], f_all.at[it, me], f_send.at[it], f_recv.at[it, me // 2], peer)

    def f_local(it):
        return pltpu.make_async_copy(f_own.at[it], f_all.at[it, me], f_recv.at[it, me // 2])

    def from_others(buffer, sem):
        part = buffer.at[pl.ds(0, buffer.shape[0] - 1)]
        return pltpu.make_async_copy(part, part, sem)

    def f_pair(it, pp):
        both = f_all.at[it, pl.ds(2 * pp, 2)]
        pltpu.make_async_copy(both, both, f_recv.at[it, pp]).wait()
        return jnp.concatenate([f_all[it, 2 * pp], f_all[it, 2 * pp + 1]], axis=1)

    def sweep(it):
        image = img[...]
        left = pieces(image)

        def row_at(t):
            dy = side - 1 - t
            return lax.rem(my_y + (dy + 1) // 2 * (2 * (dy % 2) - 1) + side, side)

        def row_of_factor(t):
            first = row_at(t) * side
            for k in range(side):
                at = pl.ds(pl.multiple_of((first + k) * piece, piece), piece)
                s_out[it, first + k] = fold(dot(left, g[:, at]) + dot(left, e[:, at]), rank)

        def send_row(t):
            for dx in range(side):
                s_copy(it, row_at(t) * side + lax.rem(my_x + 2 + dx, side)).start()

        def next_row(t, carry):
            send_row(t - 1)
            row_of_factor(t)
            return carry

        row_of_factor(0)
        wide = jnp.concatenate([left, jnp.zeros((96, left.shape[1]), BF16)], axis=0)
        terms = fold(dot_nt(left, wide), rank)
        gram_in[it, me] = terms + pltpu.roll(terms, 128 - rank, 1) + pltpu.roll(terms, 128 - 2 * rank, 1)
        lax.fori_loop(1, side, next_row, 0)
        for dx in range(1, side):
            s_copy(it, my_y * side + lax.rem(my_x + dx, side)).start()
        for peer in others()[::-1]:
            gram_copy(it, peer).start()
        from_others(s_in.at[it], s_recv.at[it]).wait()
        total = s_out[it, me]
        for peer in others():
            total += s_in[it, peer]
        f_own[it] = total
        for peer in others():
            f_copy(it, peer).start()
        f_local(it).start()
        from_others(gram_in.at[it], gram_recv.at[it]).wait()
        gram = gram_in[it, 0]
        for p in range(1, n_fsdp):
            gram += gram_in[it, p]
        inv[...] = inverse_cholesky(gram, rank)

    load_q.wait()

    def first_image(c, image):
        for copy in loads(c):
            copy.wait()
        at = columns(c)
        start = pieces(q[:, at])
        g_t[at, :] = g[:, at].T
        e_t[at, :] = e[:, at].T
        return image + dot(start, g_t[at, :]) + dot(start, e_t[at, :])

    zero = jnp.zeros((4 * rank, g.shape[0]), F32)
    img[...] = fold(lax.fori_loop(0, pairs, first_image, zero), rank)
    pl.semaphore_wait(barrier, n_fsdp + n_rep - 2)
    sweep(0)

    def second_image(pp, image):
        factor = pieces(apply_inverse(inv[...], f_pair(0, pp), rank))
        at = columns(pp)
        return image + dot(factor, g_t[at, :]) + dot(factor, e_t[at, :])

    img[...] = fold(over_pairs(second_image, zero), rank)
    sweep(1)

    def to_replica(src, dst, send, recv, peer):
        return pltpu.make_async_remote_copy(
            src_ref=src, dst_ref=dst, send_sem=send, recv_sem=recv, device_id={"replica": peer}, device_id_type=MESH
        )

    def row_copy(peer):
        return to_replica(z_rows.at[rep], z_rows.at[rep], zr_send, zr_recv, peer)

    def factor_copy(peer):
        return to_replica(f_all.at[1, pl.ds(2 * peer, 2)], z_fac.at[rep], zf_send, zf_recv, peer)

    rows_t = apply_inverse(inv[...], img[...], rank)
    z_rows[rep] = rows_t
    for t in range(1, n_rep):
        row_copy(lax.rem(rep + t, n_rep)).start()
    hi, mid = halves(rows_t)
    left = jnp.concatenate([hi, hi, mid, mid], axis=0).T.astype(BF16)

    def forward(pp, carry):
        factor = apply_inverse(inv[...], f_pair(1, pp), rank)
        f_all[1, 2 * pp] = factor[:, :piece]
        f_all[1, 2 * pp + 1] = factor[:, piece:]

        @pl.when(pp != rep)
        def _():
            factor_copy(pp).start()

        return carry

    def error(pp, carry):
        hi, mid = halves(jnp.concatenate([f_all[1, 2 * pp], f_all[1, 2 * pp + 1]], axis=1))
        right = jnp.concatenate([hi, mid, hi, mid], axis=0).astype(BF16)
        at = columns(pp)
        ne_ref[0, :, at] = (g[:, at].astype(F32) + e[:, at].astype(F32) - dot(left, right)).astype(BF16)
        return carry

    over_pairs(forward, 0)
    lax.fori_loop(0, pairs, error, 0)
    z_fac[rep] = f_all[1, pl.ds(2 * rep, 2)]
    from_others(z_rows, zr_recv).wait()
    from_others(z_fac, zf_recv).wait()

    for it in range(2):
        from_others(gram_in.at[it], gram_send.at[it]).wait()
        from_others(s_out.at[it], s_send.at[it]).wait()
        from_others(f_all.at[it], f_send.at[it]).wait()
    from_others(z_rows, zr_send).wait()
    from_others(z_fac, zf_send).wait()


def finish(ne, z_rows, z_fac, ne_hbm, up_hbm, up, sems):
    n_rep, rank, rows = z_rows.shape
    piece = z_fac.shape[3]
    blocks = sems.shape[0] - 1
    height = rows // blocks
    copies = []
    for b in range(blocks):
        at = pl.ds(b * height, height)
        copies.append(pltpu.make_async_copy(ne.at[0, at], ne_hbm.at[0, at], sems.at[b]))
        copies[-1].start()
    hi, mid = halves(z_rows[...].reshape(n_rep * rank, rows))
    left = jnp.concatenate([hi, hi, mid], axis=0).T.astype(BF16)
    for k in range(2):
        hi, mid = halves(z_fac[:, k].reshape(n_rep * rank, piece))
        right = jnp.concatenate([hi, mid, hi], axis=0).astype(BF16)
        up[:, k * piece : (k + 1) * piece] = (dot(left, right) * (1.0 / n_rep)).astype(BF16)
    copies.append(pltpu.make_async_copy(up, up_hbm, sems.at[blocks]))
    copies[-1].start()
    for copy in copies:
        copy.wait()


def shards(n_rep, n_fsdp, outer_grad, error_prev, q_init):
    rank, cols = q_init.shape
    rows = outer_grad.shape[1]
    piece = cols // n_fsdp
    side = math.isqrt(n_fsdp)
    dma = pltpu.SemaphoreType.DMA
    vmem = pl.BlockSpec(memory_space=pltpu.VMEM)
    hbm = pl.BlockSpec(memory_space=pltpu.HBM)
    parts = pl.pallas_call(
        functools.partial(kernel, n_rep, n_fsdp, side),
        out_shape=[
            pltpu.VMEM((1, rows, cols), BF16),
            pltpu.VMEM((n_rep, rank, rows), F32),
            pltpu.VMEM((n_rep, 2, rank, piece), F32),
        ],
        in_specs=[hbm] * 3,
        out_specs=[vmem] * 3,
        scratch_shapes=[
            pltpu.VMEM((rows, cols), BF16),
            pltpu.VMEM((rows, cols), BF16),
            pltpu.VMEM((cols, rows), BF16),
            pltpu.VMEM((cols, rows), BF16),
            pltpu.VMEM((rank, cols), F32),
            pltpu.VMEM((rank, rows), F32),
            pltpu.VMEM((rank, 128), F32),
            pltpu.VMEM((2, n_fsdp, rank, 128), F32),
            pltpu.VMEM((2, n_fsdp, rank, piece), F32),
            pltpu.VMEM((2, n_fsdp, rank, piece), F32),
            pltpu.VMEM((2, rank, piece), F32),
            pltpu.VMEM((2, n_fsdp, rank, piece), F32),
            dma((1 + n_fsdp,)),
            dma((2,)),
            dma((2,)),
            dma((2,)),
            dma((2,)),
            dma((2,)),
            dma((2, n_fsdp // 2)),
            dma,
            dma,
            dma,
            dma,
        ],
        compiler_params=pltpu.CompilerParams(
            collective_id=0, has_side_effects=True, vmem_limit_bytes=VMEM_LIMIT
        ),
    )(*(pltpu.with_memory_space_constraint(x, pltpu.HBM) for x in (outer_grad, error_prev, q_init)))
    new_error, update = pl.pallas_call(
        finish,
        out_shape=[pltpu.HBM((1, rows, cols), BF16), pltpu.HBM((rows, cols // n_rep), BF16)],
        in_specs=[vmem] * 3,
        out_specs=[hbm] * 2,
        scratch_shapes=[pltpu.VMEM((rows, cols // n_rep), BF16), dma((9,))],
        compiler_params=pltpu.CompilerParams(vmem_limit_bytes=16 << 20),
    )(*(pltpu.with_memory_space_constraint(x, pltpu.VMEM) for x in parts))
    return update, new_error


VMEM_LIMIT = 46 << 20


def solution(mesh):
    n_rep, n_fsdp = mesh.shape["replica"], mesh.shape["fsdp"]
    return jax.shard_map(
        functools.partial(shards, n_rep, n_fsdp),
        mesh=mesh,
        in_specs=(P("replica", "fsdp", None), P("replica", "fsdp", None), P()),
        out_specs=(P("fsdp", "replica"), P("replica", "fsdp", None)),
        check_vma=False,
    )
```

```python
import functools
import math

import jax
import jax.numpy as jnp
from jax import lax
from jax.experimental import pallas as pl
from jax.experimental.pallas import tpu as pltpu
from jax.sharding import PartitionSpec as P

F32, BF16 = jnp.float32, jnp.bfloat16
NT = (((1,), (1,)), ((), ()))
MESH = pl.DeviceIdType.MESH


def dot(a, b):
    return jnp.dot(a, b, preferred_element_type=F32)


def dot_nt(a, b, **kw):
    return lax.dot_general(a, b, NT, preferred_element_type=F32, **kw)


def pieces(x):
    hi = x.astype(BF16).astype(F32)
    rest = x - hi
    mid = rest.astype(BF16).astype(F32)
    return jnp.concatenate([hi, mid, rest - mid, jnp.zeros_like(x)], axis=0).astype(BF16)


def fold(x, rank):
    return x[:rank] + x[rank : 2 * rank] + x[2 * rank : 3 * rank]


def inverse_cholesky(gram, rank):
    row = lax.broadcasted_iota(jnp.int32, gram.shape, 0)
    lane = lax.broadcasted_iota(jnp.int32, gram.shape, 1)

    def step(k, aug):
        top = jnp.sum(jnp.where(row == k, aug, 0.0), axis=0, keepdims=True)
        side = jnp.sum(jnp.where(lane == k, aug, 0.0), axis=1, keepdims=True)
        scale = lax.rsqrt(jnp.sum(jnp.where(row == k, side, 0.0), axis=0, keepdims=True))
        pivot = top * scale
        return jnp.where(row == k, pivot, jnp.where(row > k, aug - (side * scale) * pivot, aug))

    aug = jnp.where(lane < rank, gram, jnp.where(lane == row + rank, 1.0, 0.0))
    return lax.fori_loop(0, rank, step, aug)


def apply_inverse(aug, x, rank):
    out = aug[:, rank : rank + 1] * x[0:1]
    for k in range(1, rank):
        out += aug[:, rank + k : rank + k + 1] * x[k : k + 1]
    return out


def halves(x):
    hi = x.astype(BF16).astype(F32)
    return hi, x - hi


def kernel(
    n_rep, n_fsdp, side, g_hbm, e_hbm, q_hbm, ne_ref, z_rows, z_fac,
    g, e, g_t, e_t, q, img, inv, gram_in, s_out, s_in, f_own, f_all,
    load_sem, gram_send, gram_recv, s_send, s_recv, f_send, f_recv, zr_send, zr_recv, zf_send, zf_recv,
):
    rank, cols = q.shape
    piece = cols // n_fsdp
    pairs, pair = n_fsdp // 2, 2 * piece
    rep, me = lax.axis_index("replica"), lax.axis_index("fsdp")
    my_y, my_x = me // side, me % side

    def columns(pp):
        return pl.ds(pl.multiple_of(pp * pair, pair), pair)

    def loads(c):
        at = columns(c)
        return (
            pltpu.make_async_copy(g_hbm.at[0, :, at], g.at[:, at], load_sem.at[2 * c]),
            pltpu.make_async_copy(e_hbm.at[0, :, at], e.at[:, at], load_sem.at[2 * c + 1]),
        )

    load_q = pltpu.make_async_copy(q_hbm, q, load_sem.at[2 * pairs])
    load_q.start()
    for c in range(pairs):
        for copy in loads(c):
            copy.start()

    barrier = pltpu.get_barrier_semaphore()
    for t in range(1, n_fsdp):
        pl.semaphore_signal(barrier, inc=1, device_id={"fsdp": lax.rem(me + t, n_fsdp)}, device_id_type=MESH)
    for t in range(1, n_rep):
        pl.semaphore_signal(barrier, inc=1, device_id={"replica": lax.rem(rep + t, n_rep)}, device_id_type=MESH)

    def far(step, size):
        return min(step, size - step)

    def others():
        steps = [(dy, dx) for dy in range(side) for dx in range(side) if dy or dx]
        steps.sort(key=lambda s: (far(s[0], side), far(s[1], side)))
        return [lax.rem(my_y + dy, side) * side + lax.rem(my_x + dx, side) for dy, dx in steps]

    def over_pairs(step, carry):
        half = side // 2

        def run(rows, count, carry):
            def at(j, carry):
                row = lax.rem(my_y + rows(lax.rem(j, count)) + side, side)
                return step(row * half + lax.rem(my_x // 2 + j // count, half), carry)

            return lax.fori_loop(0, count * half, at, carry)

        carry = run(lambda j: 0 * j, 1, carry)
        carry = run(lambda j: 1 - 2 * j, 2, carry)
        return run(lambda j: 2 + j, side - 3, carry)

    def to_peer(src, dst, send, recv, peer):
        return pltpu.make_async_remote_copy(
            src_ref=src, dst_ref=dst, send_sem=send, recv_sem=recv, device_id={"fsdp": peer}, device_id_type=MESH
        )

    def gram_copy(it, peer):
        return to_peer(gram_in.at[it, me], gram_in.at[it, me], gram_send.at[it], gram_recv.at[it], peer)

    def s_copy(it, peer):
        return to_peer(s_out.at[it, peer], s_in.at[it, me], s_send.at[it], s_recv.at[it], peer)

    def f_copy(it, peer):
        return to_peer(f_own.at[it], f_all.at[it, me], f_send.at[it], f_recv.at[it, me // 2], peer)

    def f_local(it):
        return pltpu.make_async_copy(f_own.at[it], f_all.at[it, me], f_recv.at[it, me // 2])

    def from_others(buffer, sem):
        part = buffer.at[pl.ds(0, buffer.shape[0] - 1)]
        return pltpu.make_async_copy(part, part, sem)

    def f_pair(it, pp):
        both = f_all.at[it, pl.ds(2 * pp, 2)]
        pltpu.make_async_copy(both, both, f_recv.at[it, pp]).wait()
        return jnp.concatenate([f_all[it, 2 * pp], f_all[it, 2 * pp + 1]], axis=1)

    def sweep(it):
        image = img[...]
        left = pieces(image)

        def row_at(t):
            dy = side - 1 - t
            return lax.rem(my_y + (dy + 1) // 2 * (2 * (dy % 2) - 1) + side, side)

        def piece_of_factor(p):
            at = pl.ds(pl.multiple_of(p * piece, piece), piece)
            s_out[it, p] = fold(dot(left, g[:, at]) + dot(left, e[:, at]), rank)

        def row_of_factor(t):
            for k in range(side):
                piece_of_factor(row_at(t) * side + k)

        def send_row(t):
            for dx in range(side):
                s_copy(it, row_at(t) * side + lax.rem(my_x + 2 + dx, side)).start()

        def next_row(t, carry):
            send_row(t - 1)
            row_of_factor(t)
            return carry

        row_of_factor(0)
        wide = jnp.concatenate([left, jnp.zeros((96, left.shape[1]), BF16)], axis=0)
        terms = fold(dot_nt(left, wide), rank)
        gram_in[it, me] = terms + pltpu.roll(terms, 128 - rank, 1) + pltpu.roll(terms, 128 - 2 * rank, 1)
        def last_row(j, carry):
            pl.when(j == 0)(lambda: send_row(side - 2))
            dx = 2 + j - 3 * (j // 2) - 2 * (j // 3)
            peer = my_y * side + lax.rem(my_x + dx, side)
            piece_of_factor(peer)
            pl.when(peer != me)(lambda: s_copy(it, peer).start())
            return carry

        lax.fori_loop(1, side - 1, next_row, 0)
        lax.fori_loop(0, side, last_row, 0)
        for peer in others()[::-1]:
            gram_copy(it, peer).start()
        from_others(s_in.at[it], s_recv.at[it]).wait()
        total = s_out[it, me]
        for peer in others():
            total += s_in[it, peer]
        f_own[it] = total
        for peer in others():
            f_copy(it, peer).start()
        f_local(it).start()
        from_others(gram_in.at[it], gram_recv.at[it]).wait()
        gram = gram_in[it, 0]
        for p in range(1, n_fsdp):
            gram += gram_in[it, p]
        inv[...] = inverse_cholesky(gram, rank)

    load_q.wait()

    def first_image(c, image):
        for copy in loads(c):
            copy.wait()
        at = columns(c)
        start = pieces(q[:, at])
        g_t[at, :] = g[:, at].T
        e_t[at, :] = e[:, at].T
        return image + dot(start, g_t[at, :]) + dot(start, e_t[at, :])

    zero = jnp.zeros((4 * rank, g.shape[0]), F32)
    img[...] = fold(lax.fori_loop(0, pairs, first_image, zero), rank)
    pl.semaphore_wait(barrier, n_fsdp + n_rep - 2)
    sweep(0)

    def second_image(pp, image):
        factor = pieces(apply_inverse(inv[...], f_pair(0, pp), rank))
        at = columns(pp)
        return image + dot(factor, g_t[at, :]) + dot(factor, e_t[at, :])

    img[...] = fold(over_pairs(second_image, zero), rank)
    sweep(1)

    def to_replica(src, dst, send, recv, peer):
        return pltpu.make_async_remote_copy(
            src_ref=src, dst_ref=dst, send_sem=send, recv_sem=recv, device_id={"replica": peer}, device_id_type=MESH
        )

    def row_copy(peer):
        return to_replica(z_rows.at[rep], z_rows.at[rep], zr_send, zr_recv, peer)

    def factor_copy(peer):
        return to_replica(f_all.at[1, pl.ds(2 * peer, 2)], z_fac.at[rep], zf_send, zf_recv, peer)

    rows_t = apply_inverse(inv[...], img[...], rank)
    z_rows[rep] = rows_t
    for t in range(1, n_rep):
        row_copy(lax.rem(rep + t, n_rep)).start()
    hi, mid = halves(rows_t)
    left = jnp.concatenate([hi, hi, mid, mid], axis=0).T.astype(BF16)

    def forward(pp, carry):
        factor = apply_inverse(inv[...], f_pair(1, pp), rank)
        f_all[1, 2 * pp] = factor[:, :piece]
        f_all[1, 2 * pp + 1] = factor[:, piece:]

        @pl.when(pp != rep)
        def _():
            factor_copy(pp).start()

        return carry

    def error(pp, carry):
        hi, mid = halves(jnp.concatenate([f_all[1, 2 * pp], f_all[1, 2 * pp + 1]], axis=1))
        right = jnp.concatenate([hi, mid, hi, mid], axis=0).astype(BF16)
        at = columns(pp)
        ne_ref[0, :, at] = (g[:, at].astype(F32) + e[:, at].astype(F32) - dot(left, right)).astype(BF16)
        return carry

    over_pairs(forward, 0)
    lax.fori_loop(0, pairs, error, 0)
    z_fac[rep] = f_all[1, pl.ds(2 * rep, 2)]
    for it in range(2):
        from_others(gram_in.at[it], gram_send.at[it]).wait()
        from_others(s_out.at[it], s_send.at[it]).wait()
        from_others(f_all.at[it], f_send.at[it]).wait()
    from_others(z_rows, zr_send).wait()
    from_others(z_rows, zr_recv).wait()
    from_others(z_fac, zf_recv).wait()

    from_others(z_fac, zf_send).wait()


def finish(ne, z_rows, z_fac, ne_hbm, up_hbm, up, sems):
    n_rep, rank, rows = z_rows.shape
    piece = z_fac.shape[3]
    blocks = sems.shape[0] - 1
    height = rows // blocks
    copies = []
    for b in range(blocks):
        at = pl.ds(b * height, height)
        copies.append(pltpu.make_async_copy(ne.at[0, at], ne_hbm.at[0, at], sems.at[b]))
        copies[-1].start()
    hi, mid = halves(z_rows[...].reshape(n_rep * rank, rows))
    left = jnp.concatenate([hi, hi, mid], axis=0).T.astype(BF16)
    for k in range(2):
        hi, mid = halves(z_fac[:, k].reshape(n_rep * rank, piece))
        right = jnp.concatenate([hi, mid, hi], axis=0).astype(BF16)
        up[:, k * piece : (k + 1) * piece] = (dot(left, right) * (1.0 / n_rep)).astype(BF16)
    copies.append(pltpu.make_async_copy(up, up_hbm, sems.at[blocks]))
    copies[-1].start()
    for copy in copies:
        copy.wait()


def shards(n_rep, n_fsdp, outer_grad, error_prev, q_init):
    rank, cols = q_init.shape
    rows = outer_grad.shape[1]
    piece = cols // n_fsdp
    side = math.isqrt(n_fsdp)
    dma = pltpu.SemaphoreType.DMA
    vmem = pl.BlockSpec(memory_space=pltpu.VMEM)
    hbm = pl.BlockSpec(memory_space=pltpu.HBM)
    parts = pl.pallas_call(
        functools.partial(kernel, n_rep, n_fsdp, side),
        out_shape=[
            pltpu.VMEM((1, rows, cols), BF16),
            pltpu.VMEM((n_rep, rank, rows), F32),
            pltpu.VMEM((n_rep, 2, rank, piece), F32),
        ],
        in_specs=[hbm] * 3,
        out_specs=[vmem] * 3,
        scratch_shapes=[
            pltpu.VMEM((rows, cols), BF16),
            pltpu.VMEM((rows, cols), BF16),
            pltpu.VMEM((cols, rows), BF16),
            pltpu.VMEM((cols, rows), BF16),
            pltpu.VMEM((rank, cols), F32),
            pltpu.VMEM((rank, rows), F32),
            pltpu.VMEM((rank, 128), F32),
            pltpu.VMEM((2, n_fsdp, rank, 128), F32),
            pltpu.VMEM((2, n_fsdp, rank, piece), F32),
            pltpu.VMEM((2, n_fsdp, rank, piece), F32),
            pltpu.VMEM((2, rank, piece), F32),
            pltpu.VMEM((2, n_fsdp, rank, piece), F32),
            dma((1 + n_fsdp,)),
            dma((2,)),
            dma((2,)),
            dma((2,)),
            dma((2,)),
            dma((2,)),
            dma((2, n_fsdp // 2)),
            dma,
            dma,
            dma,
            dma,
        ],
        compiler_params=pltpu.CompilerParams(
            collective_id=0, has_side_effects=True, vmem_limit_bytes=VMEM_LIMIT
        ),
    )(*(pltpu.with_memory_space_constraint(x, pltpu.HBM) for x in (outer_grad, error_prev, q_init)))
    new_error, update = pl.pallas_call(
        finish,
        out_shape=[pltpu.HBM((1, rows, cols), BF16), pltpu.HBM((rows, cols // n_rep), BF16)],
        in_specs=[vmem] * 3,
        out_specs=[hbm] * 2,
        scratch_shapes=[pltpu.VMEM((rows, cols // n_rep), BF16), dma((9,))],
        compiler_params=pltpu.CompilerParams(vmem_limit_bytes=16 << 20),
    )(*(pltpu.with_memory_space_constraint(x, pltpu.VMEM) for x in parts))
    return update, new_error


VMEM_LIMIT = 46 << 20


def solution(mesh):
    n_rep, n_fsdp = mesh.shape["replica"], mesh.shape["fsdp"]
    return jax.shard_map(
        functools.partial(shards, n_rep, n_fsdp),
        mesh=mesh,
        in_specs=(P("replica", "fsdp", None), P("replica", "fsdp", None), P()),
        out_specs=(P("fsdp", "replica"), P("replica", "fsdp", None)),
        check_vma=False,
    )
```

```python
import functools
import math

import jax
import jax.numpy as jnp
from jax import lax
from jax.experimental import pallas as pl
from jax.experimental.pallas import tpu as pltpu
from jax.sharding import PartitionSpec as P

F32, BF16 = jnp.float32, jnp.bfloat16
NT = (((1,), (1,)), ((), ()))
MESH = pl.DeviceIdType.MESH


def dot(a, b):
    return jnp.dot(a, b, preferred_element_type=F32)


def dot_nt(a, b, **kw):
    return lax.dot_general(a, b, NT, preferred_element_type=F32, **kw)


def pieces(x):
    hi = x.astype(BF16).astype(F32)
    rest = x - hi
    mid = rest.astype(BF16).astype(F32)
    return jnp.concatenate([hi, mid, rest - mid, jnp.zeros_like(x)], axis=0).astype(BF16)


def fold(x, rank):
    return x[:rank] + x[rank : 2 * rank] + x[2 * rank : 3 * rank]


def inverse_cholesky(gram, rank):
    row = lax.broadcasted_iota(jnp.int32, gram.shape, 0)
    lane = lax.broadcasted_iota(jnp.int32, gram.shape, 1)

    def step(k, aug):
        top = jnp.sum(jnp.where(row == k, aug, 0.0), axis=0, keepdims=True)
        side = jnp.sum(jnp.where(lane == k, aug, 0.0), axis=1, keepdims=True)
        scale = lax.rsqrt(jnp.sum(jnp.where(row == k, side, 0.0), axis=0, keepdims=True))
        pivot = top * scale
        return jnp.where(row == k, pivot, jnp.where(row > k, aug - (side * scale) * pivot, aug))

    aug = jnp.where(lane < rank, gram, jnp.where(lane == row + rank, 1.0, 0.0))
    return lax.fori_loop(0, rank, step, aug)


def apply_inverse(aug, x, rank):
    out = aug[:, rank : rank + 1] * x[0:1]
    for k in range(1, rank):
        out += aug[:, rank + k : rank + k + 1] * x[k : k + 1]
    return out


def halves(x):
    hi = x.astype(BF16).astype(F32)
    return hi, x - hi


def kernel(
    n_rep, n_fsdp, side, g_hbm, e_hbm, q_hbm, ne_ref, z_rows, z_fac,
    g, e, g_t, e_t, q, img, inv, gram_in, s_out, s_in, f_own, f_all,
    load_sem, gram_send, gram_recv, s_send, s_recv, f_send, f_recv, zr_send, zr_recv, zf_send, zf_recv,
):
    rank, cols = q.shape
    piece = cols // n_fsdp
    pairs, pair = n_fsdp // 2, 2 * piece
    rep, me = lax.axis_index("replica"), lax.axis_index("fsdp")
    my_y, my_x = me // side, me % side

    def columns(pp):
        return pl.ds(pl.multiple_of(pp * pair, pair), pair)

    def loads(c):
        at = columns(c)
        return (
            pltpu.make_async_copy(g_hbm.at[0, :, at], g.at[:, at], load_sem.at[2 * c]),
            pltpu.make_async_copy(e_hbm.at[0, :, at], e.at[:, at], load_sem.at[2 * c + 1]),
        )

    load_q = pltpu.make_async_copy(q_hbm, q, load_sem.at[2 * pairs])
    load_q.start()
    for c in range(pairs):
        for copy in loads(c):
            copy.start()

    barrier = pltpu.get_barrier_semaphore()
    for t in range(1, n_rep):
        pl.semaphore_signal(barrier, inc=1, device_id={"replica": lax.rem(rep + t, n_rep)}, device_id_type=MESH)

    def far(step, size):
        return min(step, size - step)

    def others():
        steps = [(dy, dx) for dy in range(side) for dx in range(side) if dy or dx]
        steps.sort(key=lambda s: (far(s[0], side), far(s[1], side)))
        return [lax.rem(my_y + dy, side) * side + lax.rem(my_x + dx, side) for dy, dx in steps]

    def over_pairs(step, carry):
        half = side // 2

        def run(rows, count, carry):
            def at(j, carry):
                row = lax.rem(my_y + rows(lax.rem(j, count)) + side, side)
                return step(row * half + lax.rem(my_x // 2 + j // count, half), carry)

            return lax.fori_loop(0, count * half, at, carry)

        carry = run(lambda j: 0 * j, 1, carry)
        carry = run(lambda j: 1 - 2 * j, 2, carry)
        return run(lambda j: 2 + j, side - 3, carry)

    def to_peer(src, dst, send, recv, peer):
        return pltpu.make_async_remote_copy(
            src_ref=src, dst_ref=dst, send_sem=send, recv_sem=recv, device_id={"fsdp": peer}, device_id_type=MESH
        )

    def gram_copy(it, peer):
        return to_peer(gram_in.at[it, me], gram_in.at[it, me], gram_send.at[it], gram_recv.at[it], peer)

    def s_copy(it, peer):
        return to_peer(s_out.at[it, peer], s_in.at[it, me], s_send.at[it], s_recv.at[it], peer)

    def f_copy(it, peer):
        return to_peer(f_own.at[it], f_all.at[it, me], f_send.at[it], f_recv.at[it, me // 2], peer)

    def f_local(it):
        return pltpu.make_async_copy(f_own.at[it], f_all.at[it, me], f_recv.at[it, me // 2])

    def from_others(buffer, sem):
        part = buffer.at[pl.ds(0, buffer.shape[0] - 1)]
        return pltpu.make_async_copy(part, part, sem)

    def f_pair(it, pp):
        both = f_all.at[it, pl.ds(2 * pp, 2)]
        pltpu.make_async_copy(both, both, f_recv.at[it, pp]).wait()
        return jnp.concatenate([f_all[it, 2 * pp], f_all[it, 2 * pp + 1]], axis=1)

    def sweep(it):
        image = img[...]
        left = pieces(image)

        def row_at(t):
            dy = side - 1 - t
            return lax.rem(my_y + (dy + 1) // 2 * (2 * (dy % 2) - 1) + side, side)

        def piece_of_factor(p):
            at = pl.ds(pl.multiple_of(p * piece, piece), piece)
            s_out[it, p] = fold(dot(left, g[:, at]) + dot(left, e[:, at]), rank)

        def row_of_factor(t):
            for k in range(side):
                piece_of_factor(row_at(t) * side + k)

        def send_row(t):
            for dx in range(side):
                s_copy(it, row_at(t) * side + lax.rem(my_x + 2 + dx, side)).start()

        def next_row(t, carry):
            send_row(t - 1)
            row_of_factor(t)
            return carry

        row_of_factor(0)
        wide = jnp.concatenate([left, jnp.zeros((96, left.shape[1]), BF16)], axis=0)
        terms = fold(dot_nt(left, wide), rank)
        gram_in[it, me] = terms + pltpu.roll(terms, 128 - rank, 1) + pltpu.roll(terms, 128 - 2 * rank, 1)
        def last_row(j, carry):
            pl.when(j == 0)(lambda: send_row(side - 2))
            dx = 2 + j - 3 * (j // 2) - 2 * (j // 3)
            peer = my_y * side + lax.rem(my_x + dx, side)
            piece_of_factor(peer)
            pl.when(peer != me)(lambda: s_copy(it, peer).start())
            return carry

        lax.fori_loop(1, side - 1, next_row, 0)
        lax.fori_loop(0, side, last_row, 0)
        for peer in others()[::-1]:
            gram_copy(it, peer).start()
        from_others(s_in.at[it], s_recv.at[it]).wait()
        total = s_out[it, me]
        for peer in others():
            total += s_in[it, peer]
        f_own[it] = total
        for peer in others():
            f_copy(it, peer).start()
        f_local(it).start()
        from_others(gram_in.at[it], gram_recv.at[it]).wait()
        gram = gram_in[it, 0]
        for p in range(1, n_fsdp):
            gram += gram_in[it, p]
        inv[...] = inverse_cholesky(gram, rank)

    load_q.wait()

    def first_image(c, image):
        for copy in loads(c):
            copy.wait()
        at = columns(c)
        start = pieces(q[:, at])
        g_t[at, :] = g[:, at].T
        e_t[at, :] = e[:, at].T
        return image + dot(start, g_t[at, :]) + dot(start, e_t[at, :])

    share = (n_fsdp - 1) // 3

    def greet_and_image(c, image):
        for t in range(share):
            peer = lax.rem(me + 1 + c * share + t, n_fsdp)
            pl.semaphore_signal(barrier, inc=1, device_id={"fsdp": peer}, device_id_type=MESH)
        return first_image(c, image)

    zero = jnp.zeros((4 * rank, g.shape[0]), F32)
    image = lax.fori_loop(0, 3, greet_and_image, zero)
    img[...] = fold(lax.fori_loop(3, pairs, first_image, image), rank)
    pl.semaphore_wait(barrier, n_fsdp + n_rep - 2)
    sweep(0)

    def second_image(pp, image):
        factor = pieces(apply_inverse(inv[...], f_pair(0, pp), rank))
        at = columns(pp)
        return image + dot(factor, g_t[at, :]) + dot(factor, e_t[at, :])

    img[...] = fold(over_pairs(second_image, zero), rank)
    sweep(1)

    def to_replica(src, dst, send, recv, peer):
        return pltpu.make_async_remote_copy(
            src_ref=src, dst_ref=dst, send_sem=send, recv_sem=recv, device_id={"replica": peer}, device_id_type=MESH
        )

    def row_copy(peer):
        return to_replica(z_rows.at[rep], z_rows.at[rep], zr_send, zr_recv, peer)

    def factor_copy(peer):
        return to_replica(f_all.at[1, pl.ds(2 * peer, 2)], z_fac.at[rep], zf_send, zf_recv, peer)

    rows_t = apply_inverse(inv[...], img[...], rank)
    z_rows[rep] = rows_t
    for t in range(1, n_rep):
        row_copy(lax.rem(rep + t, n_rep)).start()
    hi, mid = halves(rows_t)
    left = jnp.concatenate([hi, hi, mid, mid], axis=0).T.astype(BF16)

    def forward(pp, carry):
        factor = apply_inverse(inv[...], f_pair(1, pp), rank)
        f_all[1, 2 * pp] = factor[:, :piece]
        f_all[1, 2 * pp + 1] = factor[:, piece:]

        @pl.when(pp != rep)
        def _():
            factor_copy(pp).start()

        return carry

    def error(pp, carry):
        hi, mid = halves(jnp.concatenate([f_all[1, 2 * pp], f_all[1, 2 * pp + 1]], axis=1))
        right = jnp.concatenate([hi, mid, hi, mid], axis=0).astype(BF16)
        at = columns(pp)
        ne_ref[0, :, at] = (g[:, at].astype(F32) + e[:, at].astype(F32) - dot(left, right)).astype(BF16)
        return carry

    over_pairs(forward, 0)
    lax.fori_loop(0, pairs, error, 0)
    z_fac[rep] = f_all[1, pl.ds(2 * rep, 2)]
    for it in range(2):
        from_others(gram_in.at[it], gram_send.at[it]).wait()
        from_others(s_out.at[it], s_send.at[it]).wait()
        from_others(f_all.at[it], f_send.at[it]).wait()
    from_others(z_rows, zr_send).wait()
    from_others(z_rows, zr_recv).wait()
    from_others(z_fac, zf_recv).wait()

    from_others(z_fac, zf_send).wait()


def finish(ne, z_rows, z_fac, ne_hbm, up_hbm, up, sems):
    n_rep, rank, rows = z_rows.shape
    piece = z_fac.shape[3]
    blocks = sems.shape[0] - 1
    height = rows // blocks
    copies = []
    for b in range(blocks):
        at = pl.ds(b * height, height)
        copies.append(pltpu.make_async_copy(ne.at[0, at], ne_hbm.at[0, at], sems.at[b]))
        copies[-1].start()
    hi, mid = halves(z_rows[...].reshape(n_rep * rank, rows))
    left = jnp.concatenate([hi, hi, mid], axis=0).T.astype(BF16)
    for k in range(2):
        hi, mid = halves(z_fac[:, k].reshape(n_rep * rank, piece))
        right = jnp.concatenate([hi, mid, hi], axis=0).astype(BF16)
        up[:, k * piece : (k + 1) * piece] = (dot(left, right) * (1.0 / n_rep)).astype(BF16)
    copies.append(pltpu.make_async_copy(up, up_hbm, sems.at[blocks]))
    copies[-1].start()
    for copy in copies:
        copy.wait()


def shards(n_rep, n_fsdp, outer_grad, error_prev, q_init):
    rank, cols = q_init.shape
    rows = outer_grad.shape[1]
    piece = cols // n_fsdp
    side = math.isqrt(n_fsdp)
    dma = pltpu.SemaphoreType.DMA
    vmem = pl.BlockSpec(memory_space=pltpu.VMEM)
    hbm = pl.BlockSpec(memory_space=pltpu.HBM)
    parts = pl.pallas_call(
        functools.partial(kernel, n_rep, n_fsdp, side),
        out_shape=[
            pltpu.VMEM((1, rows, cols), BF16),
            pltpu.VMEM((n_rep, rank, rows), F32),
            pltpu.VMEM((n_rep, 2, rank, piece), F32),
        ],
        in_specs=[hbm] * 3,
        out_specs=[vmem] * 3,
        scratch_shapes=[
            pltpu.VMEM((rows, cols), BF16),
            pltpu.VMEM((rows, cols), BF16),
            pltpu.VMEM((cols, rows), BF16),
            pltpu.VMEM((cols, rows), BF16),
            pltpu.VMEM((rank, cols), F32),
            pltpu.VMEM((rank, rows), F32),
            pltpu.VMEM((rank, 128), F32),
            pltpu.VMEM((2, n_fsdp, rank, 128), F32),
            pltpu.VMEM((2, n_fsdp, rank, piece), F32),
            pltpu.VMEM((2, n_fsdp, rank, piece), F32),
            pltpu.VMEM((2, rank, piece), F32),
            pltpu.VMEM((2, n_fsdp, rank, piece), F32),
            dma((1 + n_fsdp,)),
            dma((2,)),
            dma((2,)),
            dma((2,)),
            dma((2,)),
            dma((2,)),
            dma((2, n_fsdp // 2)),
            dma,
            dma,
            dma,
            dma,
        ],
        compiler_params=pltpu.CompilerParams(
            collective_id=0, has_side_effects=True, vmem_limit_bytes=VMEM_LIMIT
        ),
    )(*(pltpu.with_memory_space_constraint(x, pltpu.HBM) for x in (outer_grad, error_prev, q_init)))
    new_error, update = pl.pallas_call(
        finish,
        out_shape=[pltpu.HBM((1, rows, cols), BF16), pltpu.HBM((rows, cols // n_rep), BF16)],
        in_specs=[vmem] * 3,
        out_specs=[hbm] * 2,
        scratch_shapes=[pltpu.VMEM((rows, cols // n_rep), BF16), dma((9,))],
        compiler_params=pltpu.CompilerParams(vmem_limit_bytes=16 << 20),
    )(*(pltpu.with_memory_space_constraint(x, pltpu.VMEM) for x in parts))
    return update, new_error


VMEM_LIMIT = 46 << 20


def solution(mesh):
    n_rep, n_fsdp = mesh.shape["replica"], mesh.shape["fsdp"]
    return jax.shard_map(
        functools.partial(shards, n_rep, n_fsdp),
        mesh=mesh,
        in_specs=(P("replica", "fsdp", None), P("replica", "fsdp", None), P()),
        out_specs=(P("fsdp", "replica"), P("replica", "fsdp", None)),
        check_vma=False,
    )
```
